128 devices in a mesh: dp: 8 (over y, z_hi), fsdp: 16 (over x, z_lo, core).
Axes of the slice: x: 4, y: 4, z: 4 (z_hi: 2, z_lo: 2; z = z_hi * 2 + z_lo), core: 2. Of those that a mesh axis runs over, the one named last changes fastest.
Arguments:
- q_in: bfloat16 [16384, 4096], P(('dp', 'fsdp')), may hold values from -6.5 to 6.5
- k_in: bfloat16 [16384, 512], P(('dp', 'fsdp')), may hold values from -6.5 to 6.5
- v_in: bfloat16 [16384, 512], P(('dp', 'fsdp')), may hold values from -6 to 6
- grad_out: bfloat16 [16384, 4096], P(('dp', 'fsdp')), may hold values from -6 to 6
- q_gain: float32 [128], replicated, may hold values from 0.6 to 5.5
- k_gain: float32 [128], replicated, may hold values from 0.6 to 5.5
- shift_plan: int32 [16, 8], P('fsdp'), may hold values from 0 to 7, each once within a row
- segment_ids: int32 [8, 2048], P('dp', 'fsdp'), may hold values from 0 to 7, never falling along the last dimension, each value on 1 to 1024 neighbouring positions
Outputs:
- dq_in: bfloat16 [16384, 4096], P(('dp', 'fsdp'))
- dk_in: bfloat16 [16384, 512], P(('dp', 'fsdp'))
- dv_in: bfloat16 [16384, 512], P(('dp', 'fsdp'))
- q_gain_grad: float32 [128], replicated
- k_gain_grad: float32 [128], replicated
The draws below stay inside these ranges and needn't reach their ends.
Inputs may be any that keep to these rules, and one draw needn't show every extreme that they name: `shift_plan`: each row of the swap plan names every number from 0 to 7 once. `segment_ids`: each group's ids never fall along its rows; each rollout holds 1 to 1024 tokens and one holds exactly 1024.
All inputs are finite; a program needn't handle non-finite values.
Results may differ from the reference program's by a relative error of at most 0.01.
The reference program's roundings to bfloat16 on the way count: a program that leaves them out, or rounds other values in their place, can miss the bound.
Values may be sent and summed in bfloat16 or wider, within the bound.
No kernel may reach another device: no remote copies, remote signals or barrier semaphores. Data moves between devices by JAX's collectives and lax.ppermute only.
A program may use at most 192 MiB of HBM per device.

```python
import math
import jax
import jax.numpy as jnp
import numpy as np
from jax import lax

HQ = 32
HK = 4
HD = 128
TOK_DEV = 128
DOCS = 8
TOKG = 2048
ROWS = 16384
MAXLEN = 1024
N_DP = 8
N_FSDP = 16


def shared_keys(key):
    base = jnp.clip(jax.random.normal(key, (ROWS, HK * HD), jnp.float32), -6.0, 6.0)
    return base


def draw_k_in(key, part):
    base = shared_keys(key)
    return base.astype(jnp.bfloat16)


def draw_q_in(key, part):
    key = jax.random.fold_in(key, 9)
    own_key = jax.random.fold_in(key, 0)
    own = jnp.clip(jax.random.normal(own_key, (ROWS, HK, HQ // HK, HD), jnp.float32), -6.0, 6.0)
    return own.reshape(ROWS, HQ * HD).astype(jnp.bfloat16)


def draw_q_gain(key, part):
    key = jax.random.fold_in(key, 21)
    return jax.random.uniform(key, (HD,), jnp.float32, 0.6, 1.6)


def draw_k_gain(key, part):
    key = jax.random.fold_in(key, 23)
    return jax.random.uniform(key, (HD,), jnp.float32, 0.6, 1.6)


def levels(rng, extent, pieces, low, top_value):
    def one(dim, parts):
        heights = jax.random.uniform(jax.random.fold_in(jax.random.fold_in(rng, 6), dim), (parts,), jnp.float32, low / len(pieces), top_value / len(pieces))
        return jnp.repeat(jnp.exp(heights), extent[dim] // parts).reshape((-1,) + (1,) * (len(extent) - dim - 1))

    level = one(*pieces[0])
    for cut in pieces[1:]:
        level = level * one(*cut)
    return level


def split_up(count, total, bound, slope):
    loads = [(1 << 20) // math.isqrt(rank ** slope) + 1 for rank in range(2, count + 1)]
    surplus, counts = total - bound - (count - 1), [1] * (count - 1)
    while surplus > 0:
        candidates = [i for i in range(count - 1) if counts[i] < bound]
        mass, remaining = sum([loads[i] for i in candidates]), surplus
        for i in candidates:
            more = min(bound - counts[i], max(1, remaining * loads[i] // mass), surplus)
            counts[i] = counts[i] + more
            surplus = surplus - more
    return np.array([bound] + counts)


def ragged(key, count, total, limit, lean):
    if count == 2:
        one = jax.random.randint(key, (), max(1, total - limit), min(limit, total - 1) + 1)
        return jnp.stack([one, total - one])
    lengths = jnp.asarray(split_up(count, total, limit, lean), jnp.int32)
    twos = (count - 1) // 2
    donor, taker = lengths[1:1 + 2 * twos:2], lengths[2:2 + 2 * twos:2]
    margin = jnp.minimum(donor - 1, limit - taker)
    moved = jax.random.randint(jax.random.fold_in(key, 1), (twos,), 0, 1 << 20) % (margin + 1)
    lengths = lengths.at[1:1 + 2 * twos:2].set(donor - moved).at[2:2 + 2 * twos:2].set(taker + moved)
    return lengths[jax.random.permutation(jax.random.fold_in(key, 2), count)]


def gaussian(key, shape, scale, most, cuts=(), held_as=jnp.bfloat16):
    level = levels(key, shape, cuts, -0.22, 0.18) if cuts else 1.0
    drawn = jax.random.normal(key, shape, jnp.float32) * scale * level
    return jnp.minimum(jnp.maximum(drawn, -most), most).astype(held_as)


def setup_inputs(seed: int = 0) -> dict:
    keys = jax.random.split(jax.random.key(seed), 9)
    q_in = draw_q_in(jax.random.fold_in(keys[8], 71), 0)
    k_in = draw_k_in(jax.random.fold_in(keys[8], 71), 0)
    v_in = gaussian(keys[2], (ROWS, HK * HD), 1.0, 6.0, ((0, 128),))
    grad_out = gaussian(keys[3], (ROWS, HQ * HD), 1.0, 6.0, ((0, 128),))
    q_gain = draw_q_gain(jax.random.fold_in(keys[8], 71), 0)
    k_gain = draw_k_gain(jax.random.fold_in(keys[8], 71), 0)
    shift_plan = jax.vmap(lambda own: jax.random.permutation(own, N_DP))(jax.random.split(keys[6], N_FSDP)).reshape((N_FSDP, N_DP)).astype(jnp.int32)
    segment_ids = jax.vmap(lambda own: jnp.searchsorted(jnp.cumsum(ragged(own, DOCS, TOKG, MAXLEN, 2)), jnp.arange(TOKG), side="right"))(jax.random.split(keys[7], N_DP)).reshape((N_DP, TOKG)).astype(jnp.int32)
    return {"q_in": q_in, "k_in": k_in, "v_in": v_in, "grad_out": grad_out, "q_gain": q_gain, "k_gain": k_gain, "shift_plan": shift_plan, "segment_ids": segment_ids}


THETA = 1000000.0
EPS = 1e-06
NEG = -1e+30

def run_positions(seg):
    count = seg.shape[0]
    index = jnp.arange(count, dtype=jnp.int32)
    boundary = jnp.concatenate([jnp.ones((1,), jnp.bool_), seg[1:] != seg[:-1]])
    start = lax.cummax(jnp.where(boundary, index, jnp.int32(0)), axis=0)
    return index - start

def rope_tables(positions, head_dim):
    half = head_dim // 2
    freq = THETA ** (-(jnp.arange(half, dtype=jnp.float32) * 2.0 / head_dim))
    angle = positions.astype(jnp.float32)[:, None] * freq[None, :]
    return (jnp.cos(angle), jnp.sin(angle))

def norm_rope(x, gain, cosine, sine):
    values = x.astype(jnp.float32)
    rscale = lax.rsqrt(lax.optimization_barrier(jnp.mean(values * values, axis=-1, keepdims=True)) + EPS)
    normed = values * rscale * gain
    half = x.shape[-1] // 2
    first, second = (normed[..., :half], normed[..., half:])
    cos_b, sin_b = (cosine[:, None, :], sine[:, None, :])
    turned = jnp.concatenate([first * cos_b - second * sin_b, second * cos_b + first * sin_b], axis=-1)
    return (turned.astype(jnp.bfloat16), rscale)

def norm_rope_back(grad, x, gain, rscale, cosine, sine):
    half = grad.shape[-1] // 2
    cos_b, sin_b = (cosine[:, None, :], sine[:, None, :])
    upper, lower = (grad[..., :half], grad[..., half:])
    dnormed = jnp.concatenate([upper * cos_b + lower * sin_b, lower * cos_b - upper * sin_b], axis=-1)
    values = x.astype(jnp.float32)
    gain_term = lax.optimization_barrier(jnp.sum(dnormed * values * rscale, axis=(0, 1)))
    inner = dnormed * gain
    dx = rscale * inner - values * rscale ** 3 * lax.optimization_barrier(jnp.mean(inner * values, axis=-1, keepdims=True))
    return (dx.astype(jnp.bfloat16), gain_term)

def swap_rows(x, shift_plan):
    run = TOK_DEV // N_DP
    blocks = x.reshape(N_DP, N_FSDP, N_DP, run, x.shape[1])
    group = jnp.arange(N_DP, dtype=jnp.int32)[:, None, None]
    source = (group - shift_plan[None, :, :]) % N_DP
    shard = jnp.arange(N_FSDP, dtype=jnp.int32)[None, :, None]
    slot = jnp.arange(N_DP, dtype=jnp.int32)[None, None, :]
    return blocks[source, shard, slot].reshape(x.shape)

def to_bf16(x):
    rounded = lax.optimization_barrier(x.astype(jnp.bfloat16))
    return rounded.astype(jnp.float32)

def group_backward(q_rot, k_rot, v_rows, g_rows, seg):
    count = q_rot.shape[0]
    width = min(512, count)
    nblk = count // width
    share = HQ // HK
    scale = HD ** (-0.5)
    q_all = q_rot.astype(jnp.float32).reshape(count, HK, share, HD)
    g_all = g_rows.astype(jnp.float32).reshape(count, HK, share, HD)
    k_all = k_rot.astype(jnp.float32)
    v_all = v_rows.astype(jnp.float32)
    index = jnp.arange(count, dtype=jnp.int32)
    dk_list = [jnp.zeros((width, HK, HD), jnp.float32) for step in range(nblk)]
    dv_list = [jnp.zeros((width, HK, HD), jnp.float32) for step in range(nblk)]
    dq_list = []
    for qblk in range(nblk):
        qsl = slice(qblk * width, (qblk + 1) * width)
        q_blk, g_blk = (q_all[qsl], g_all[qsl])
        top = jnp.full((HK, share, width), NEG, jnp.float32)
        total = jnp.zeros((HK, share, width), jnp.float32)
        acc = jnp.zeros((HK, share, width, HD), jnp.float32)
        masks = []
        for kblk in range(qblk + 1):
            ksl = slice(kblk * width, (kblk + 1) * width)
            allowed = (seg[qsl][:, None] == seg[ksl][None, :]) & (index[ksl][None, :] <= index[qsl][:, None])
            masks.append(allowed)
            score = jnp.einsum('qksd,tkd->ksqt', q_blk, k_all[ksl]) * scale
            score = jnp.where(allowed, score, NEG)
            new_top = jnp.maximum(top, lax.optimization_barrier(jnp.max(score, axis=-1)))
            weight = jnp.where(allowed, jnp.exp(score - new_top[..., None]), 0.0)
            fade = jnp.exp(top - new_top)
            total = total * fade + lax.optimization_barrier(jnp.sum(weight, axis=-1))
            acc = acc * fade[..., None] + jnp.einsum('ksqt,tkd->ksqd', weight, v_all[ksl])
            top = new_top
        lse = top + jnp.log(total)
        out = acc / total[..., None]
        delta = jnp.einsum('qksd,ksqd->ksq', g_blk, out)
        dq = jnp.zeros((HK, share, width, HD), jnp.float32)
        for kblk in range(qblk + 1):
            ksl = slice(kblk * width, (kblk + 1) * width)
            allowed = masks[kblk]
            score = jnp.einsum('qksd,tkd->ksqt', q_blk, k_all[ksl]) * scale
            prob = jnp.where(allowed, jnp.exp(score - lse[..., None]), 0.0)
            prob_b = to_bf16(prob)
            dprob = jnp.einsum('qksd,tkd->ksqt', g_blk, v_all[ksl])
            dscore = to_bf16(prob * (dprob - delta[..., None]))
            dq = dq + jnp.einsum('ksqt,tkd->ksqd', dscore, k_all[ksl]) * scale
            dk_list[kblk] = dk_list[kblk] + jnp.einsum('ksqt,qksd->tkd', dscore, q_blk) * scale
            dv_list[kblk] = dv_list[kblk] + jnp.einsum('ksqt,qksd->tkd', prob_b, g_blk)
        dq_list.append(jnp.transpose(dq, (2, 0, 1, 3)).reshape(width, HQ, HD))
    return (jnp.concatenate(dq_list, 0), jnp.concatenate(dk_list, 0), jnp.concatenate(dv_list, 0))

def reference(q_in, k_in, v_in, grad_out, q_gain, k_gain, shift_plan, segment_ids):
    q_swap = swap_rows(q_in, shift_plan)
    k_swap = swap_rows(k_in, shift_plan)
    v_swap = swap_rows(v_in, shift_plan)
    dq_parts, dk_parts, dv_parts = ([], [], [])
    q_term = jnp.zeros((HD,), jnp.float32)
    k_term = jnp.zeros((HD,), jnp.float32)
    for group in range(N_DP):
        rows = slice(group * TOKG, (group + 1) * TOKG)
        seg = segment_ids[group]
        cosine, sine = rope_tables(run_positions(seg), HD)
        q_raw = q_swap[rows].reshape(TOKG, HQ, HD)
        k_raw = k_swap[rows].reshape(TOKG, HK, HD)
        q_rot, q_scale = norm_rope(q_raw, q_gain, cosine, sine)
        k_rot, k_scale = norm_rope(k_raw, k_gain, cosine, sine)
        v_rows = v_swap[rows].reshape(TOKG, HK, HD)
        dq_rot, dk_rot, dv = group_backward(q_rot, k_rot, v_rows, grad_out[rows], seg)
        dq, q_part = norm_rope_back(dq_rot, q_raw, q_gain, q_scale, cosine, sine)
        dk, k_part = norm_rope_back(dk_rot, k_raw, k_gain, k_scale, cosine, sine)
        q_term = q_term + q_part
        k_term = k_term + k_part
        dq_parts.append(dq.reshape(TOKG, HQ * HD))
        dk_parts.append(dk.reshape(TOKG, HK * HD))
        dv_parts.append(dv.reshape(TOKG, HK * HD).astype(jnp.bfloat16))
    return (jnp.concatenate(dq_parts, 0), jnp.concatenate(dk_parts, 0), jnp.concatenate(dv_parts, 0), q_term, k_term)
```

```python
import math

import jax
import jax.numpy as jnp
from jax import lax
from jax.experimental import pallas as pl
from jax.experimental.pallas import tpu as pltpu
from jax.sharding import Mesh, PartitionSpec as P

THETA = 1000000.0
EPS = 1e-06
NEG = -1e30
HD = 128
RUN = 16
TILE = 128
BACK = 8
WIN = (BACK + 1) * TILE
ALLW = (BACK + 2) * TILE
SCALE = HD**-0.5
TO_EXP2 = SCALE * math.log2(math.e)
BF = jnp.bfloat16
F32 = jnp.float32
VM = pl.BlockSpec(memory_space=pltpu.VMEM)
SM = pl.BlockSpec(memory_space=pltpu.SMEM)
PARAMS = pltpu.CompilerParams(vmem_limit_bytes=44 * 1024 * 1024)


def sincos(angle):
    turns = jnp.round(angle * (2.0 / math.pi))
    r = ((angle - turns * 1.5703125) - turns * 4.837512969970703e-4) - turns * 7.549789948768648e-8
    r2 = r * r
    sin_r = r + r * r2 * (-1.6666654611e-1 + r2 * (8.3321608736e-3 - 1.9515295891e-4 * r2))
    cos_r = 1.0 - 0.5 * r2 + r2 * r2 * (
        4.166664568298827e-2 + r2 * (-1.388731625493765e-3 + 2.443315711809948e-5 * r2)
    )
    quarter = turns.astype(jnp.int32)
    swap = (quarter & 1) == 1
    s = jnp.where(swap, cos_r, sin_r)
    c = jnp.where(swap, sin_r, cos_r)
    s = jnp.where((quarter & 2) == 2, -s, s)
    c = jnp.where(((quarter + 1) & 2) == 2, -c, c)
    return s, c


def inv_rms(x):
    return lax.rsqrt(jnp.sum(x * x, axis=-1, keepdims=True) * (1.0 / HD) + EPS)


def rope(x, tc, ts):
    return x * tc + pltpu.roll(x, HD // 2, 1) * ts


def rope_back(x, tc, ts):
    return x * tc - pltpu.roll(x, HD // 2, 1) * ts


def norm_back(dn, x, rs, gain):
    w = dn * gain
    return rs * w - x * (rs * rs * rs) * (jnp.sum(w * x, axis=-1, keepdims=True) * (1.0 / HD))


def fold(x, op):
    return op(x.reshape(x.shape[0] // 8, 8, x.shape[1]), axis=0)


def dot(a, b):
    return jnp.dot(a, b, preferred_element_type=F32)


def send_kernel(plan_ref, who_ref, q_ref, k_ref, v_ref, out_ref):
    groups = plan_ref.shape[1]
    wide_q, wide_k = q_ref.shape[1] // 2, k_ref.shape[1] // 2
    for r in range(groups):
        to = lax.rem(who_ref[0] + plan_ref[0, r], groups)
        rows = slice(r * RUN, (r + 1) * RUN)
        for a in range(2):
            out_ref[2 * to + a, :, :wide_q] = q_ref[rows, a * wide_q : (a + 1) * wide_q]
            out_ref[2 * to + a, :, wide_q : wide_q + wide_k] = k_ref[rows, a * wide_k : (a + 1) * wide_k]
            out_ref[2 * to + a, :, wide_q + wide_k :] = v_ref[rows, a * wide_k : (a + 1) * wide_k]


def keys_kernel(src_ref, recv_ref, seg_ref, out_ref):
    for b in range(2):
        for r in range(8):
            rows = slice(b * TILE + r * RUN, b * TILE + (r + 1) * RUN)
            out_ref[rows, :] = recv_ref[src_ref[b * 8 + r]]
    ids = (seg_ref[...] + 1).astype(F32)
    row = jnp.concatenate([ids, jnp.zeros_like(ids)], axis=1)
    out_ref[2 * TILE :, :] = jnp.broadcast_to(row, (RUN, row.shape[1])).astype(BF)


def main_kernel(
    core_ref, src_ref, recv_ref, kv4, kv3, kv2, kv1, kv0, g_own, g_sib, freq_ref, qg_ref, kg_ref,
    dq_own, dq_sib, out1, out2, out3, out4, own_ref, tco_ref, tso_ref, gains_ref,
    tc, ts, kr, kt, vs, xq, q8, g8, bias, sc, dp, pb, db, dk_acc, dv_acc,
):
    core = core_ref[0]
    kvs = (kv4, kv3, kv2, kv1, kv0)
    lane = lax.broadcasted_iota(jnp.int32, (TILE, TILE), 1)
    sub = lax.broadcasted_iota(jnp.int32, (TILE, TILE), 0)
    ids = [kv[2 * TILE :, : 2 * TILE].astype(F32)[:8] for kv in kvs]
    begin = jnp.zeros_like(ids[-1])
    for v in range(1, 9):
        less = sum(jnp.where(one < v, 1.0, 0.0) for one in ids)
        begin = begin + jnp.where(ids[-1] == v, jnp.sum(less, axis=1, keepdims=True), 0.0)
    first = begin[0:1, 0:1]
    subf = sub.astype(F32)
    qgain, kgain = qg_ref[...], kg_ref[...]
    for blk in range(BACK + 2):
        rows = slice(blk * TILE, (blk + 1) * TILE)
        if blk < BACK:
            start = first
        else:
            mine = slice((blk - BACK) * TILE, (blk - BACK + 1) * TILE)
            start = jnp.broadcast_to(begin[0:1, mine], (TILE, TILE)).T
        sine, cosine = sincos((subf + float(blk * TILE) - start) * freq_ref[...])
        sine = jnp.where(lane < HD // 2, -sine, sine)
        tc[rows, :] = cosine
        ts[rows, :] = sine
        if blk >= BACK:
            tco_ref[mine, :] = cosine
            tso_ref[mine, :] = sine
        ref, part = kvs[blk // 2], slice((blk % 2) * TILE, (blk % 2 + 1) * TILE)
        for j in range(2):
            x = ref[part, j * HD : (j + 1) * HD].astype(F32)
            turned = rope(x * inv_rms(x) * kgain, cosine, sine)
            kr[j, rows, :] = turned.astype(BF)
            kt[j, :, rows] = turned.T.astype(BF)
            vs[j, rows, :] = ref[part, (2 + j) * HD : (3 + j) * HD]
    dk_acc[...] = jnp.zeros_like(dk_acc)
    dv_acc[...] = jnp.zeros_like(dv_acc)
    q_term = jnp.zeros((8, HD), F32)
    for turn, (g_ref, dq_ref) in enumerate(((g_own, dq_own), (g_sib, dq_sib))):
        tile = core if turn == 0 else 1 - core
        base = pl.multiple_of(tile * TILE, TILE)
        for r in range(8):
            xq[r * RUN : (r + 1) * RUN, :] = recv_ref[src_ref[tile * 8 + r]]
        st = jnp.where(tile == 0, begin[0:1, :TILE], begin[0:1, TILE:]) - (tile * TILE).astype(F32)
        for kb in range(BACK + 1):
            ok = (subf + float(kb * TILE)) >= st
            if kb == BACK:
                ok = ok & (sub <= lane)
            bias[kb * TILE : (kb + 1) * TILE, :] = jnp.where(ok, 0.0, NEG)
        own_rows = pl.ds(pl.multiple_of(BACK * TILE + base, TILE), TILE)

        def head(j, q_term):
            def pair(hp, q_term):
                raws, scales, qts, gts = [], [], [], []
                for hh in range(2):
                    cols = pl.ds(pl.multiple_of((j * 8 + hp * 2 + hh) * HD, HD), HD)
                    x = xq[:, cols].astype(F32)
                    rs = inv_rms(x)
                    turned = rope(x * rs * qgain, tc[own_rows, :], ts[own_rows, :])
                    grad = g_ref[:, cols]
                    slot = pl.ds(pl.multiple_of((hp * 2 + hh) * TILE, TILE), TILE)
                    q8[slot, :] = turned.astype(BF)
                    g8[slot, :] = grad
                    raws.append(x)
                    scales.append(rs)
                    qts.append(turned.T.astype(BF))
                    gts.append(grad.astype(F32).T.astype(BF))
                qt = jnp.concatenate(qts, axis=1)
                gt = jnp.concatenate(gts, axis=1)
                top = jnp.full((8, 2 * TILE), NEG, F32)
                for kb in range(BACK + 1):
                    rows = slice(kb * TILE, (kb + 1) * TILE)
                    keys = pl.ds(pl.multiple_of(base + kb * TILE, TILE), TILE)
                    b = bias[rows, :]
                    s = dot(kr[j, keys, :], qt) + jnp.concatenate([b, b], axis=1)
                    sc[rows, :] = s
                    top = jnp.maximum(top, fold(s, jnp.max))
                    dp[rows, :] = dot(vs[j, keys, :], gt)
                top = jnp.max(top, axis=0, keepdims=True) * TO_EXP2
                total = jnp.zeros((8, 2 * TILE), F32)
                inner = jnp.zeros((8, 2 * TILE), F32)
                for kb in range(BACK + 1):
                    rows = slice(kb * TILE, (kb + 1) * TILE)
                    e = jnp.exp2(sc[rows, :] * TO_EXP2 - top)
                    sc[rows, :] = e
                    total = total + fold(e, jnp.sum)
                    inner = inner + fold(e * dp[rows, :], jnp.sum)
                inv = 1.0 / jnp.sum(total, axis=0, keepdims=True)
                delta = jnp.sum(inner, axis=0, keepdims=True) * inv
                two = pl.ds(pl.multiple_of(hp * 2 * TILE, 2 * TILE), 2 * TILE)
                for kb in range(BACK + 1):
                    rows = slice(kb * TILE, (kb + 1) * TILE)
                    p = sc[rows, :] * inv
                    pb[rows, two] = p.astype(BF)
                    db[rows, two] = (p * (dp[rows, :] - delta)).astype(BF)
                dqt = dot(kt[j, :, pl.ds(base, WIN)], db[:, two]) * SCALE
                for hh in range(2):
                    cols = pl.ds(pl.multiple_of((j * 8 + hp * 2 + hh) * HD, HD), HD)
                    dn = rope_back(dqt[:, hh * TILE : (hh + 1) * TILE].T, tc[own_rows, :], ts[own_rows, :])
                    x, rs = raws[hh], scales[hh]
                    q_term = q_term + fold(dn * x * rs, jnp.sum)
                    dq_ref[:, cols] = norm_back(dn, x, rs, qgain).astype(BF)
                return q_term

            q_term = lax.fori_loop(0, 4, pair, q_term)
            keys = pl.ds(base, WIN)
            dv_acc[j, keys, :] += dot(pb[...], g8[...])
            dk_acc[j, keys, :] += dot(db[...], q8[...])
            return q_term

        q_term = lax.fori_loop(0, 2, head, q_term)
    k_term = jnp.zeros((8, HD), F32)
    outs = (out4, out3, out2, out1)
    for blk in range(BACK + 2):
        rows = slice(blk * TILE, (blk + 1) * TILE)
        part = slice((blk % 2) * TILE, (blk % 2 + 1) * TILE)
        for j in range(2):
            dk = dk_acc[j, rows, :] * SCALE
            dv = dv_acc[j, rows, :]
            x = kvs[blk // 2][part, j * HD : (j + 1) * HD].astype(F32)
            dn = rope_back(dk, tc[rows, :], ts[rows, :])
            k_term = k_term + fold(dn * x * inv_rms(x), jnp.sum)
            dk_cols, dv_cols = slice(j * HD, (j + 1) * HD), slice((2 + j) * HD, (3 + j) * HD)
            if blk < BACK:
                outs[blk // 2][part, dk_cols] = dk.astype(BF)
                outs[blk // 2][part, dv_cols] = dv.astype(BF)
            else:
                own_ref[part, dk_cols] = dk
                own_ref[part, dv_cols] = dv
    gains_ref[0:1, :] = jnp.sum(q_term, axis=0, keepdims=True)
    gains_ref[1:2, :] = jnp.sum(k_term, axis=0, keepdims=True)


def finish_kernel(core_ref, own_ref, r1, r2, r3, r4, kv_ref, tc_ref, ts_ref, kg_ref, mine_ref, other_ref, both):
    core = core_ref[0]
    for b in range(2):
        rows = slice(b * TILE, (b + 1) * TILE)
        total = own_ref[rows, :]
        for r in (r1, r2, r3, r4):
            total = total + r[rows, :].astype(F32)
        for j in range(2):
            cols = slice(j * HD, (j + 1) * HD)
            x = kv_ref[rows, cols].astype(F32)
            dn = rope_back(total[:, cols], tc_ref[rows, :], ts_ref[rows, :])
            both[b, :, cols] = norm_back(dn, x, inv_rms(x), kg_ref[...]).astype(BF)
        both[b, :, 2 * HD :] = total[:, 2 * HD :].astype(BF)
    mine_ref[...] = both[core]
    other_ref[...] = both[1 - core]


def body(q_in, k_in, v_in, grad_out, q_gain, k_gain, shift_plan, segment_ids):
    groups = lax.axis_size("dp")
    chips = lax.axis_size("chip")
    member = lax.axis_index("dp").astype(jnp.int32)
    core = lax.axis_index("core").astype(jnp.int32)
    core1 = core.reshape(1)
    wide = q_in.shape[1] // 2
    sds = jax.ShapeDtypeStruct

    def to_sibling(x):
        return lax.ppermute(x, "core", [(0, 1), (1, 0)])

    def by_core(mine, other, axis):
        return jnp.where(
            core == 0,
            jnp.concatenate([mine, other], axis=axis),
            jnp.concatenate([other, mine], axis=axis),
        )

    packed = pl.pallas_call(
        send_kernel,
        out_shape=sds((2 * groups, RUN, 2560), BF),
        in_specs=[SM, SM, VM, VM, VM],
        out_specs=VM,
        compiler_params=PARAMS,
        name="pack_runs",
    )(shift_plan, member.reshape(1), q_in, k_in, v_in)
    small = jnp.concatenate([shift_plan, segment_ids], axis=1)
    small2 = by_core(small, to_sibling(small), 0)
    g_sib = to_sibling(lax.dynamic_slice_in_dim(grad_out, (1 - core) * wide, wide, 1))
    recv = lax.all_to_all(packed, ("dp", "core"), 0, 0, tiled=True)
    src = 2 * ((member - small2[:, :groups]) % groups) + jnp.arange(2, dtype=jnp.int32)[:, None]
    src = src.reshape(2 * groups)
    segs = small2[:, groups:].reshape(1, 2 * TILE)
    kv0 = pl.pallas_call(
        keys_kernel,
        out_shape=sds((2 * TILE + RUN, 4 * HD), BF),
        grid=(1,),
        in_specs=[SM, pl.BlockSpec((2 * groups, RUN, 4 * HD), lambda i: (0, 0, 4)), VM],
        out_specs=VM,
        compiler_params=PARAMS,
        name="own_keys",
    )(src, recv, segs)
    kv = [lax.ppermute(kv0, "chip", [(i, i + d) for i in range(chips - d)]) for d in range(1, 5)]
    half = jnp.arange(HD // 2, dtype=F32)
    freq = THETA ** (-(half * 2.0 / HD))
    freq = jnp.concatenate([freq, freq]).reshape(1, HD)
    rows2 = 2 * TILE
    res = pl.pallas_call(
        main_kernel,
        out_shape=(
            [sds((TILE, wide), BF)] * 2
            + [sds((rows2, 4 * HD), BF)] * 4
            + [sds((rows2, 4 * HD), F32)]
            + [sds((rows2, HD), F32)] * 2
            + [sds((2, HD), F32)]
        ),
        grid_spec=pltpu.PrefetchScalarGridSpec(
            num_scalar_prefetch=2,
            grid=(1,),
            in_specs=[pl.BlockSpec((2 * groups, RUN, wide), lambda i, c, s: (0, 0, 0))]
            + [VM] * 5
            + [pl.BlockSpec((TILE, wide), lambda i, c, s: (0, c[0]))]
            + [VM] * 4,
            out_specs=[VM] * 10,
            scratch_shapes=[
                pltpu.VMEM((ALLW, HD), F32),
                pltpu.VMEM((ALLW, HD), F32),
                pltpu.VMEM((2, ALLW, HD), BF),
                pltpu.VMEM((2, HD, ALLW), BF),
                pltpu.VMEM((2, ALLW, HD), BF),
                pltpu.VMEM((TILE, wide), BF),
                pltpu.VMEM((8 * TILE, HD), BF),
                pltpu.VMEM((8 * TILE, HD), BF),
                pltpu.VMEM((WIN, TILE), F32),
                pltpu.VMEM((WIN, 2 * TILE), F32),
                pltpu.VMEM((WIN, 2 * TILE), F32),
                pltpu.VMEM((WIN, 8 * TILE), BF),
                pltpu.VMEM((WIN, 8 * TILE), BF),
                pltpu.VMEM((2, ALLW, HD), F32),
                pltpu.VMEM((2, ALLW, HD), F32),
            ],
        ),
        compiler_params=PARAMS,
        name="attention_grads",
    )(
        core1, src, recv, kv[3], kv[2], kv[1], kv[0], kv0, grad_out, g_sib,
        freq, q_gain.reshape(1, HD), k_gain.reshape(1, HD),
    )
    dq_mine, dq_other, parts, own, tco, tso, gains = res[0], res[1], res[2:6], *res[6:]
    back = [
        lax.ppermute(part, "chip", [(i, i - d) for i in range(d, chips)])
        for d, part in zip(range(1, 5), parts)
    ]
    dq_got = to_sibling(dq_other)
    every = 2 * groups * chips
    spread = jnp.broadcast_to(gains.reshape(1, 1, 2 * HD), (every, 1, 2 * HD))
    terms = jnp.sum(lax.all_to_all(spread, ("dp", "chip", "core"), 0, 0, tiled=True), axis=(0, 1))
    mine, other = pl.pallas_call(
        finish_kernel,
        out_shape=[sds((TILE, 4 * HD), BF)] * 2,
        in_specs=[SM] + [VM] * 9,
        out_specs=[VM] * 2,
        scratch_shapes=[pltpu.VMEM((2, TILE, 4 * HD), BF)],
        compiler_params=PARAMS,
        name="finish_keys",
    )(core1, own, *back, kv0, tco, tso, k_gain.reshape(1, HD))
    got = to_sibling(other)
    dq = by_core(dq_mine, dq_got, 1)
    dk = by_core(mine[:, : 2 * HD], got[:, : 2 * HD], 1)
    dv = by_core(mine[:, 2 * HD :], got[:, 2 * HD :], 1)
    return dq, dk, dv, terms[:HD], terms[HD:]


def solution(mesh):
    fine = Mesh(mesh.devices.reshape(mesh.shape["dp"], -1, 2), ("dp", "chip", "core"))
    rows = P(("dp", "chip", "core"), None)
    return jax.shard_map(
        body,
        mesh=fine,
        in_specs=(rows, rows, rows, rows, P(), P(), P(("chip", "core"), None), P("dp", ("chip", "core"))),
        out_specs=(rows, rows, rows, P(), P()),
        check_vma=False,
    )
```

```python
import math

import jax
import jax.numpy as jnp
from jax import lax
from jax.experimental import pallas as pl
from jax.experimental.pallas import tpu as pltpu
from jax.sharding import Mesh, PartitionSpec as P

THETA = 1000000.0
EPS = 1e-06
NEG = -1e30
HG = 4
HD = 128
RUN = 16
TILE = 128
BACK = 8
WIN = (BACK + 1) * TILE
ALLW = (BACK + 2) * TILE
SCALE = HD**-0.5
TO_EXP2 = SCALE * math.log2(math.e)
BF = jnp.bfloat16
F32 = jnp.float32
SM = pl.BlockSpec(memory_space=pltpu.SMEM)
PARAMS = pltpu.CompilerParams(vmem_limit_bytes=48 * 1024 * 1024)


def whole(*shape):
    return pl.BlockSpec(shape, lambda i, *scalars: (0,) * len(shape))


def sincos(angle):
    turns = jnp.round(angle * (2.0 / math.pi))
    r = ((angle - turns * 1.5703125) - turns * 4.837512969970703e-4) - turns * 7.549789948768648e-8
    r2 = r * r
    sin_r = r + r * r2 * (-1.6666654611e-1 + r2 * (8.3321608736e-3 - 1.9515295891e-4 * r2))
    cos_r = 1.0 - 0.5 * r2 + r2 * r2 * (
        4.166664568298827e-2 + r2 * (-1.388731625493765e-3 + 2.443315711809948e-5 * r2)
    )
    quarter = turns.astype(jnp.int32)
    swap = (quarter & 1) == 1
    s = jnp.where(swap, cos_r, sin_r)
    c = jnp.where(swap, sin_r, cos_r)
    s = jnp.where((quarter & 2) == 2, -s, s)
    c = jnp.where(((quarter + 1) & 2) == 2, -c, c)
    return s, c


def inv_rms(x):
    return lax.rsqrt(jnp.sum(x * x, axis=-1, keepdims=True) * (1.0 / HD) + EPS)


def rope(x, tc, ts):
    return x * tc + pltpu.roll(x, HD // 2, 1) * ts


def rope_back(x, tc, ts):
    return x * tc - pltpu.roll(x, HD // 2, 1) * ts


def norm_back(dn, x, rs, gain):
    w = dn * gain
    return rs * w - x * (rs * rs * rs) * (jnp.sum(w * x, axis=-1, keepdims=True) * (1.0 / HD))


def fold(x, op):
    return op(x.reshape(x.shape[0] // 8, 8, x.shape[1]), axis=0)


def dot(a, b):
    return jnp.dot(a, b, preferred_element_type=F32)


def send_kernel(plan_ref, who_ref, q_ref, k_ref, v_ref, out_ref):
    groups = plan_ref.shape[1]
    wide_q, wide_k = q_ref.shape[1] // 2, k_ref.shape[1] // 2
    for r in range(groups):
        to = lax.rem(who_ref[0] + plan_ref[0, r], groups)
        rows = slice(r * RUN, (r + 1) * RUN)
        for a in range(2):
            out_ref[2 * to + a, :, :wide_q] = q_ref[rows, a * wide_q : (a + 1) * wide_q]
            out_ref[2 * to + a, :, wide_q : wide_q + wide_k] = k_ref[rows, a * wide_k : (a + 1) * wide_k]
            out_ref[2 * to + a, :, wide_q + wide_k :] = v_ref[rows, a * wide_k : (a + 1) * wide_k]


def keys_kernel(src_ref, recv_ref, *out_refs):
    for b in range(2):
        for r in range(8):
            rows = slice(b * TILE + r * RUN, b * TILE + (r + 1) * RUN)
            one = recv_ref[src_ref[b * 8 + r]]
            for j, out_ref in enumerate(out_refs):
                out_ref[rows, :HD] = one[:, j * HD : (j + 1) * HD]
                out_ref[rows, HD:] = one[:, (2 + j) * HD : (3 + j) * HD]


def tables_kernel(core_ref, id4, id3, id2, id1, id0, freq_ref, tc, ts, bias):
    core = core_ref[0]
    lane = lax.broadcasted_iota(jnp.int32, (TILE, TILE), 1)
    sub = lax.broadcasted_iota(jnp.int32, (TILE, TILE), 0)
    subf = sub.astype(F32)
    ids = [jnp.broadcast_to(one[...], (8, 2 * TILE)) for one in (id4, id3, id2, id1, id0)]
    begin = jnp.zeros((8, 2 * TILE), F32)
    for v in range(1, 9):
        less = sum(jnp.where(one < v, 1.0, 0.0) for one in ids)
        begin = begin + jnp.where(ids[-1] == v, jnp.sum(less, axis=1, keepdims=True), 0.0)
    for blk in range(BACK + 2):
        rows = slice(blk * TILE, (blk + 1) * TILE)
        if blk < BACK:
            start = begin[0:1, 0:1]
        else:
            mine = slice((blk - BACK) * TILE, (blk - BACK + 1) * TILE)
            start = jnp.broadcast_to(begin[0:1, mine], (TILE, TILE)).T
        sine, cosine = sincos((subf + float(blk * TILE) - start) * freq_ref[...])
        tc[rows, :] = cosine
        ts[rows, :] = jnp.where(lane < HD // 2, -sine, sine)
    for turn in range(2):
        tile = core if turn == 0 else 1 - core
        st = jnp.where(tile == 0, begin[0:1, :TILE], begin[0:1, TILE:]) - (tile * TILE).astype(F32)
        for kb in range(BACK + 1):
            ok = (subf + float(kb * TILE)) >= st
            if kb == BACK:
                ok = ok & (sub <= lane)
            bias[turn, kb * TILE : (kb + 1) * TILE, :] = jnp.where(ok, 0.0, NEG).astype(BF)


def heads_kernel(
    core_ref, src_ref, recv_ref, kv4, kv3, kv2, kv1, kv0, g_own, g_sib, tc, ts, bias, qg_ref, kg_ref,
    dq_own, dq_sib, out1, out2, out3, out4, own_ref, gains_ref,
    kr, kt, vs, xq, q8s, g8s, sc0, sc1, dp0, dp1, pb0, pb1, db0, db1, dk_acc, dv_acc,
):
    core = core_ref[0]
    kvs = (kv4, kv3, kv2, kv1, kv0)
    lane = lax.broadcasted_iota(jnp.int32, (TILE, TILE), 1)
    sub = lax.broadcasted_iota(jnp.int32, (TILE, TILE), 0)
    eye = jnp.where(sub == lane, 1.0, 0.0).astype(BF)
    qgain, kgain = qg_ref[...], kg_ref[...]
    for blk in range(BACK + 2):
        rows = slice(blk * TILE, (blk + 1) * TILE)
        ref, part = kvs[blk // 2], slice((blk % 2) * TILE, (blk % 2 + 1) * TILE)
        x = ref[part, :HD].astype(F32)
        turned = rope(x * inv_rms(x) * kgain, tc[rows, :], ts[rows, :])
        kr[rows, :] = turned.astype(BF)
        kt[:, rows] = turned.T.astype(BF)
        vs[rows, :] = ref[part, HD:]
    dk_acc[...] = jnp.zeros_like(dk_acc)
    dv_acc[...] = jnp.zeros_like(dv_acc)
    bases, own_rows = [], []
    for turn in range(2):
        tile = core if turn == 0 else 1 - core
        base = pl.multiple_of(tile * TILE, TILE)
        bases.append(base)
        own_rows.append(pl.ds(pl.multiple_of(BACK * TILE + base, TILE), TILE))
        for r in range(8):
            xq[turn, r * RUN : (r + 1) * RUN, :] = recv_ref[src_ref[tile * 8 + r]]
    gs, dqs = (g_own, g_sib), (dq_own, dq_sib)
    scs, dps, pbs, dbs = (sc0, sc1), (dp0, dp1), (pb0, pb1), (db0, db1)
    units = [(turn, h) for turn in range(2) for h in range(0, 8, HG)]

    def front(u):
        turn, h0 = units[u]
        qts, gts = [], []
        for h in range(h0, h0 + HG):
            cols = slice(h * HD, (h + 1) * HD)
            x = xq[turn, :, cols].astype(F32)
            turned = rope(x * inv_rms(x) * qgain, tc[own_rows[turn], :], ts[own_rows[turn], :])
            grad = gs[turn][:, cols]
            q8s[turn, h * TILE : (h + 1) * TILE, :] = turned.astype(BF)
            g8s[turn, h * TILE : (h + 1) * TILE, :] = grad
            qts.append(turned.T.astype(BF))
            gts.append(grad.astype(F32).T.astype(BF))
        qt = jnp.concatenate(
            [jnp.concatenate(qts, axis=1), jnp.concatenate([eye] * HG, axis=1)], axis=0
        )
        win = pl.ds(bases[turn], WIN)
        scs[u % 2][...] = dot(jnp.concatenate([kr[win, :], bias[turn]], axis=1), qt)
        dps[u % 2][...] = dot(vs[win, :], jnp.concatenate(gts, axis=1))

    def middle(u):
        sc, dp, pb, db = scs[u % 2], dps[u % 2], pbs[u % 2], dbs[u % 2]
        for lt in range(HG // 2):
            ls = slice(lt * 2 * TILE, (lt + 1) * 2 * TILE)
            top = jnp.full((8, 2 * TILE), NEG, F32)
            for kb in range(BACK + 1):
                rows = slice(kb * TILE, (kb + 1) * TILE)
                top = jnp.maximum(top, fold(sc[rows, ls], jnp.max))
            top = jnp.max(top, axis=0, keepdims=True) * TO_EXP2
            total = jnp.zeros((8, 2 * TILE), F32)
            inner = jnp.zeros((8, 2 * TILE), F32)
            for kb in range(BACK + 1):
                rows = slice(kb * TILE, (kb + 1) * TILE)
                e = jnp.exp2(sc[rows, ls] * TO_EXP2 - top)
                sc[rows, ls] = e
                total = total + fold(e, jnp.sum)
                inner = inner + fold(e * dp[rows, ls], jnp.sum)
            inv = 1.0 / jnp.sum(total, axis=0, keepdims=True)
            delta = jnp.sum(inner, axis=0, keepdims=True) * inv
            for kb in range(BACK + 1):
                rows = slice(kb * TILE, (kb + 1) * TILE)
                p = sc[rows, ls] * inv
                pb[rows, ls] = p.astype(BF)
                db[rows, ls] = (p * (dp[rows, ls] - delta)).astype(BF)

    def tail(u, q_term):
        turn, h0 = units[u]
        pb, db = pbs[u % 2], dbs[u % 2]
        keys = pl.ds(bases[turn], WIN)
        dqt = dot(kt[:, keys], db[...]) * SCALE
        for i, h in enumerate(range(h0, h0 + HG)):
            cols = slice(h * HD, (h + 1) * HD)
            dn = rope_back(
                dqt[:, i * TILE : (i + 1) * TILE].T, tc[own_rows[turn], :], ts[own_rows[turn], :]
            )
            x = xq[turn, :, cols].astype(F32)
            rs = inv_rms(x)
            q_term = q_term + fold(dn * x * rs, jnp.sum)
            dqs[turn][:, cols] = norm_back(dn, x, rs, qgain).astype(BF)
        mine = slice(h0 * TILE, (h0 + HG) * TILE)
        dv_acc[keys, :] += dot(pb[...], g8s[turn, mine, :])
        dk_acc[keys, :] += dot(db[...], q8s[turn, mine, :])
        return q_term

    q_term = jnp.zeros((8, HD), F32)
    front(0)
    for u in range(len(units)):
        if u + 1 < len(units):
            front(u + 1)
        middle(u)
        q_term = tail(u, q_term)
    k_term = jnp.zeros((8, HD), F32)
    outs = (out4, out3, out2, out1, own_ref)
    for blk in range(BACK + 2):
        rows = slice(blk * TILE, (blk + 1) * TILE)
        part = slice((blk % 2) * TILE, (blk % 2 + 1) * TILE)
        dk = dk_acc[rows, :] * SCALE
        x = kvs[blk // 2][part, :HD].astype(F32)
        dn = rope_back(dk, tc[rows, :], ts[rows, :])
        k_term = k_term + fold(dn * x * inv_rms(x), jnp.sum)
        out = outs[blk // 2]
        out[part, :HD] = dk.astype(out.dtype)
        out[part, HD:] = dv_acc[rows, :].astype(out.dtype)
    gains_ref[0:1, :] = jnp.sum(q_term, axis=0, keepdims=True)
    gains_ref[1:2, :] = jnp.sum(k_term, axis=0, keepdims=True)


def finish_kernel(core_ref, own_ref, r1, r2, r3, r4, kv_ref, tc_ref, ts_ref, kg_ref, mine_ref, other_ref, both):
    core = core_ref[0]
    for b in range(2):
        rows = slice(b * TILE, (b + 1) * TILE)
        total = own_ref[rows, :]
        for r in (r1, r2, r3, r4):
            total = total + r[rows, :].astype(F32)
        x = kv_ref[rows, :HD].astype(F32)
        dn = rope_back(total[:, :HD], tc_ref[rows, :], ts_ref[rows, :])
        both[b, :, :HD] = norm_back(dn, x, inv_rms(x), kg_ref[...]).astype(BF)
        both[b, :, HD:] = total[:, HD:].astype(BF)
    mine_ref[...] = both[core]
    other_ref[...] = both[1 - core]


def head_grads(j, core1, src, recv, kv4, kv3, kv2, kv1, kv0, grad_out, g_sib, tc, ts, bias, q_gain, k_gain):
    sds = jax.ShapeDtypeStruct
    groups, wide = recv.shape[0] // 2, 8 * HD
    rows2 = 2 * TILE
    unit = HG * TILE
    return pl.pallas_call(
        heads_kernel,
        out_shape=(
            [sds((TILE, wide), BF)] * 2
            + [sds((rows2, 2 * HD), BF)] * 4
            + [sds((rows2, 2 * HD), F32), sds((2, HD), F32)]
        ),
        grid_spec=pltpu.PrefetchScalarGridSpec(
            num_scalar_prefetch=2,
            grid=(1,),
            in_specs=[pl.BlockSpec((2 * groups, RUN, wide), lambda i, c, s: (0, 0, j))]
            + [whole(rows2, 2 * HD)] * 5
            + [pl.BlockSpec((TILE, wide), lambda i, c, s: (0, 2 * c[0] + j))]
            + [pl.BlockSpec((TILE, wide), lambda i, c, s: (0, j))]
            + [whole(ALLW, HD)] * 2
            + [whole(2, WIN, TILE)]
            + [whole(1, HD)] * 2,
            out_specs=[whole(TILE, wide)] * 2 + [whole(rows2, 2 * HD)] * 5 + [whole(2, HD)],
            scratch_shapes=[
                pltpu.VMEM((ALLW, HD), BF),
                pltpu.VMEM((HD, ALLW), BF),
                pltpu.VMEM((ALLW, HD), BF),
                pltpu.VMEM((2, TILE, wide), BF),
                pltpu.VMEM((2, wide, HD), BF),
                pltpu.VMEM((2, wide, HD), BF),
            ]
            + [pltpu.VMEM((WIN, unit), F32)] * 4
            + [pltpu.VMEM((WIN, unit), BF)] * 4
            + [pltpu.VMEM((ALLW, HD), F32)] * 2,
        ),
        compiler_params=PARAMS,
        cost_estimate=pl.CostEstimate(flops=3 * 10**9, bytes_accessed=6 * 10**6, transcendentals=3 * 10**6),
        name="head_grads",
    )(
        core1, src, recv, kv4, kv3, kv2, kv1, kv0, grad_out, g_sib, tc, ts, bias,
        q_gain.reshape(1, HD), k_gain.reshape(1, HD),
    )


def body(q_in, k_in, v_in, grad_out, q_gain, k_gain, shift_plan, segment_ids):
    groups = lax.axis_size("dp")
    chips = lax.axis_size("chip")
    member = lax.axis_index("dp").astype(jnp.int32)
    core = lax.axis_index("core").astype(jnp.int32)
    core1 = core.reshape(1)
    wide = q_in.shape[1] // 2
    rows2 = 2 * TILE
    sds = jax.ShapeDtypeStruct

    def to_sibling(x):
        return lax.ppermute(x, "core", [(0, 1), (1, 0)])

    def ahead(x, d):
        return lax.ppermute(x, "chip", [(i, i + d) for i in range(chips - d)])

    def behind(x, d):
        return lax.ppermute(x, "chip", [(i, i - d) for i in range(d, chips)])

    def by_core(mine, other, axis):
        return jnp.where(
            core == 0,
            jnp.concatenate([mine, other], axis=axis),
            jnp.concatenate([other, mine], axis=axis),
        )

    packed = pl.pallas_call(
        send_kernel,
        out_shape=sds((2 * groups, RUN, 2560), BF),
        grid=(1,),
        in_specs=[SM, SM, whole(*q_in.shape), whole(*k_in.shape), whole(*v_in.shape)],
        out_specs=whole(2 * groups, RUN, 2560),
        compiler_params=PARAMS,
        name="pack_runs",
    )(shift_plan, member.reshape(1), q_in, k_in, v_in)
    recv = lax.all_to_all(packed, ("dp", "core"), 0, 0, tiled=True)
    small = jnp.concatenate([shift_plan, segment_ids + 1], axis=1)
    small2 = by_core(small, to_sibling(small), 0)
    src = 2 * ((member - small2[:, :groups]) % groups) + jnp.arange(2, dtype=jnp.int32)[:, None]
    src = src.reshape(2 * groups)
    ids = small2[:, groups:].reshape(1, rows2)
    id_win = [ahead(ids, d) for d in range(1, 5)]
    half = jnp.arange(HD // 2, dtype=F32)
    freq = THETA ** (-(half * 2.0 / HD))
    freq = jnp.concatenate([freq, freq]).reshape(1, HD)
    tc, ts, bias = pl.pallas_call(
        tables_kernel,
        out_shape=[sds((ALLW, HD), F32), sds((ALLW, HD), F32), sds((2, WIN, TILE), BF)],
        grid=(1,),
        in_specs=[SM] + [whole(1, rows2)] * 5 + [whole(1, HD)],
        out_specs=[whole(ALLW, HD)] * 2 + [whole(2, WIN, TILE)],
        compiler_params=PARAMS,
        name="rope_tables",
    )(core1, *id_win[::-1], ids, freq)
    g_sib = to_sibling(lax.dynamic_slice_in_dim(grad_out, (1 - core) * wide, wide, 1))
    kv0 = pl.pallas_call(
        keys_kernel,
        out_shape=[sds((rows2, 2 * HD), BF)] * 2,
        grid=(1,),
        in_specs=[SM, pl.BlockSpec((2 * groups, RUN, 4 * HD), lambda i: (0, 0, 4))],
        out_specs=[whole(rows2, 2 * HD)] * 2,
        compiler_params=PARAMS,
        name="own_keys",
    )(src, recv)
    kv = [[ahead(kv0[j], d) for d in range(1, 5)] for j in range(2)]
    dq_mine, dq_got, gains, done = [], [], 0.0, []
    for j in range(2):
        mine, other, *parts, own, gain = head_grads(
            j, core1, src, recv, *kv[j][::-1], kv0[j], grad_out, g_sib, tc, ts, bias, q_gain, k_gain
        )
        back = [behind(part, d) for d, part in zip(range(1, 5), parts)]
        dq_mine.append(mine)
        dq_got.append(to_sibling(other))
        gains = gains + gain
        done.append((own, back))
    gains, dq_got[1] = lax.optimization_barrier((gains, dq_got[1]))
    every = 2 * groups * chips
    spread = jnp.broadcast_to(gains.reshape(1, 1, 2 * HD), (every, 1, 2 * HD))
    terms = jnp.sum(lax.all_to_all(spread, ("dp", "chip", "core"), 0, 0, tiled=True), axis=(0, 1))
    mine, got = [], []
    for j, (own, back) in enumerate(done):
        if j == 1:
            terms, own = lax.optimization_barrier((terms, own))
        a, b = pl.pallas_call(
            finish_kernel,
            out_shape=[sds((TILE, 2 * HD), BF)] * 2,
            grid=(1,),
            in_specs=[SM]
            + [whole(rows2, 2 * HD)] * 6
            + [pl.BlockSpec((rows2, HD), lambda i: (BACK // 2, 0))] * 2
            + [whole(1, HD)],
            out_specs=[whole(TILE, 2 * HD)] * 2,
            scratch_shapes=[pltpu.VMEM((2, TILE, 2 * HD), BF)],
            compiler_params=PARAMS,
            name="finish_keys",
        )(core1, own, *back, kv0[j], tc, ts, k_gain.reshape(1, HD))
        mine.append(a)
        got.append(to_sibling(b))

    def joined(part):
        return by_core(
            jnp.concatenate([part(one) for one in mine], axis=1),
            jnp.concatenate([part(one) for one in got], axis=1),
            1,
        )

    dq = by_core(jnp.concatenate(dq_mine, axis=1), jnp.concatenate(dq_got, axis=1), 1)
    dk = joined(lambda one: one[:, :HD])
    dv = joined(lambda one: one[:, HD:])
    return dq, dk, dv, terms[:HD], terms[HD:]


def solution(mesh):
    fine = Mesh(mesh.devices.reshape(mesh.shape["dp"], -1, 2), ("dp", "chip", "core"))
    rows = P(("dp", "chip", "core"), None)
    return jax.shard_map(
        body,
        mesh=fine,
        in_specs=(rows, rows, rows, rows, P(), P(), P(("chip", "core"), None), P("dp", ("chip", "core"))),
        out_specs=(rows, rows, rows, P(), P()),
        check_vma=False,
    )
```

```python
import math

import jax
import jax.numpy as jnp
from jax import lax
from jax.experimental import pallas as pl
from jax.experimental.pallas import tpu as pltpu
from jax.sharding import Mesh, PartitionSpec as P

THETA = 1000000.0
EPS = 1e-06
NEG = -1e30
HG = 4
HD = 128
RUN = 16
TILE = 128
BACK = 8
WIN = (BACK + 1) * TILE
ALLW = (BACK + 2) * TILE
SCALE = HD**-0.5
TO_EXP2 = SCALE * math.log2(math.e)
BF = jnp.bfloat16
F32 = jnp.float32
SM = pl.BlockSpec(memory_space=pltpu.SMEM)
PARAMS = pltpu.CompilerParams(vmem_limit_bytes=48 * 1024 * 1024)
ALL_VMEM = pltpu.CompilerParams(vmem_limit_bytes=60 * 1024 * 1024)


def whole(*shape):
    return pl.BlockSpec(shape, lambda i, *scalars: (0,) * len(shape))


def sincos(angle):
    turns = jnp.round(angle * (2.0 / math.pi))
    r = ((angle - turns * 1.5703125) - turns * 4.837512969970703e-4) - turns * 7.549789948768648e-8
    r2 = r * r
    sin_r = r + r * r2 * (-1.6666654611e-1 + r2 * (8.3321608736e-3 - 1.9515295891e-4 * r2))
    cos_r = 1.0 - 0.5 * r2 + r2 * r2 * (
        4.166664568298827e-2 + r2 * (-1.388731625493765e-3 + 2.443315711809948e-5 * r2)
    )
    quarter = turns.astype(jnp.int32)
    swap = (quarter & 1) == 1
    s = jnp.where(swap, cos_r, sin_r)
    c = jnp.where(swap, sin_r, cos_r)
    s = jnp.where((quarter & 2) == 2, -s, s)
    c = jnp.where(((quarter + 1) & 2) == 2, -c, c)
    return s, c


def inv_rms(x):
    return lax.rsqrt(jnp.sum(x * x, axis=-1, keepdims=True) * (1.0 / HD) + EPS)


def rope(x, tc, ts):
    return x * tc + pltpu.roll(x, HD // 2, 1) * ts


def rope_back(x, tc, ts):
    return x * tc - pltpu.roll(x, HD // 2, 1) * ts


def norm_back(dn, x, rs, gain):
    w = dn * gain
    return rs * w - x * (rs * rs * rs) * (jnp.sum(w * x, axis=-1, keepdims=True) * (1.0 / HD))


def fold(x, op):
    return op(x.reshape(x.shape[0] // 8, 8, x.shape[1]), axis=0)


def dot(a, b):
    return jnp.dot(a, b, preferred_element_type=F32)


def send_kernel(plan_ref, who_ref, q_ref, k_ref, v_ref, out_ref):
    groups = plan_ref.shape[1]
    wide_q, wide_k = q_ref.shape[1] // 2, k_ref.shape[1] // 2
    for r in range(groups):
        to = lax.rem(who_ref[0] + plan_ref[0, r], groups)
        rows = slice(r * RUN, (r + 1) * RUN)
        for a in range(2):
            out_ref[2 * to + a, :, :wide_q] = q_ref[rows, a * wide_q : (a + 1) * wide_q]
            out_ref[2 * to + a, :, wide_q : wide_q + wide_k] = k_ref[rows, a * wide_k : (a + 1) * wide_k]
            out_ref[2 * to + a, :, wide_q + wide_k :] = v_ref[rows, a * wide_k : (a + 1) * wide_k]


def keys_kernel(src_ref, recv_ref, out_ref):
    for b in range(2):
        for r in range(8):
            rows = slice(b * TILE + r * RUN, b * TILE + (r + 1) * RUN)
            out_ref[rows, :] = recv_ref[src_ref[b * 8 + r]]


def tables_kernel(core_ref, id4, id3, id2, id1, id0, freq_ref, tc, ts, bias):
    core = core_ref[0]
    lane = lax.broadcasted_iota(jnp.int32, (TILE, TILE), 1)
    sub = lax.broadcasted_iota(jnp.int32, (TILE, TILE), 0)
    subf = sub.astype(F32)
    ids = [jnp.broadcast_to(one[...], (8, 2 * TILE)) for one in (id4, id3, id2, id1, id0)]
    begin = jnp.zeros((8, 2 * TILE), F32)
    for v in range(1, 9):
        less = sum(jnp.where(one < v, 1.0, 0.0) for one in ids)
        begin = begin + jnp.where(ids[-1] == v, jnp.sum(less, axis=1, keepdims=True), 0.0)
    for blk in range(BACK + 2):
        rows = slice(blk * TILE, (blk + 1) * TILE)
        if blk < BACK:
            start = begin[0:1, 0:1]
        else:
            mine = slice((blk - BACK) * TILE, (blk - BACK + 1) * TILE)
            start = jnp.broadcast_to(begin[0:1, mine], (TILE, TILE)).T
        sine, cosine = sincos((subf + float(blk * TILE) - start) * freq_ref[...])
        tc[rows, :] = cosine
        ts[rows, :] = jnp.where(lane < HD // 2, -sine, sine)
    for turn in range(2):
        tile = core if turn == 0 else 1 - core
        st = jnp.where(tile == 0, begin[0:1, :TILE], begin[0:1, TILE:]) - (tile * TILE).astype(F32)
        for kb in range(BACK + 1):
            ok = (subf + float(kb * TILE)) >= st
            if kb == BACK:
                ok = ok & (sub <= lane)
            bias[turn, kb * TILE : (kb + 1) * TILE, :] = jnp.where(ok, 0.0, NEG).astype(BF)


def heads_kernel(
    core_ref, src_ref, recv_ref, kv4, kv3, kv2, kv1, kv0, g_own, g_sib, tc, ts, bias, qg_ref, kg_ref,
    dq_own, dq_sib, out1, out2, out3, out4, own_ref, gains_ref,
    kr, kt, vs, xq, q8s, g8s, sc0, sc1, dp0, dp1, pb0, pb1, db0, db1, dk_acc, dv_acc,
):
    core = core_ref[0]
    kvs = (kv4, kv3, kv2, kv1, kv0)
    lane = lax.broadcasted_iota(jnp.int32, (TILE, TILE), 1)
    sub = lax.broadcasted_iota(jnp.int32, (TILE, TILE), 0)
    eye = jnp.where(sub == lane, 1.0, 0.0).astype(BF)
    qgain, kgain = qg_ref[...], kg_ref[...]
    for blk in range(BACK + 2):
        rows = slice(blk * TILE, (blk + 1) * TILE)
        ref, part = kvs[blk // 2], slice((blk % 2) * TILE, (blk % 2 + 1) * TILE)
        for j in range(2):
            x = ref[part, j * HD : (j + 1) * HD].astype(F32)
            turned = rope(x * inv_rms(x) * kgain, tc[rows, :], ts[rows, :])
            kr[j, rows, :] = turned.astype(BF)
            kt[j, :, rows] = turned.T.astype(BF)
            vs[j, rows, :] = ref[part, (2 + j) * HD : (3 + j) * HD]
    dk_acc[...] = jnp.zeros_like(dk_acc)
    dv_acc[...] = jnp.zeros_like(dv_acc)
    bases, own_rows = [], []
    for turn in range(2):
        tile = core if turn == 0 else 1 - core
        base = pl.multiple_of(tile * TILE, TILE)
        bases.append(base)
        own_rows.append(pl.ds(pl.multiple_of(BACK * TILE + base, TILE), TILE))
        for r in range(8):
            xq[turn, r * RUN : (r + 1) * RUN, :] = recv_ref[src_ref[tile * 8 + r]]
    gs, dqs = (g_own, g_sib), (dq_own, dq_sib)
    scs, dps, pbs, dbs = (sc0, sc1), (dp0, dp1), (pb0, pb1), (db0, db1)
    units = [(turn, h) for turn in range(2) for h in range(0, 16, HG)]

    def front(u):
        turn, h0 = units[u]
        j, qts, gts = h0 // 8, [], []
        for h in range(h0, h0 + HG):
            cols = slice(h * HD, (h + 1) * HD)
            x = xq[turn, :, cols].astype(F32)
            turned = rope(x * inv_rms(x) * qgain, tc[own_rows[turn], :], ts[own_rows[turn], :])
            grad = gs[turn][:, cols]
            q8s[turn, h * TILE : (h + 1) * TILE, :] = turned.astype(BF)
            g8s[turn, h * TILE : (h + 1) * TILE, :] = grad
            qts.append(turned.T.astype(BF))
            gts.append(grad.astype(F32).T.astype(BF))
        qt = jnp.concatenate(
            [jnp.concatenate(qts, axis=1), jnp.concatenate([eye] * HG, axis=1)], axis=0
        )
        win = pl.ds(bases[turn], WIN)
        scs[u % 2][...] = dot(jnp.concatenate([kr[j, win, :], bias[turn]], axis=1), qt)
        dps[u % 2][...] = dot(vs[j, win, :], jnp.concatenate(gts, axis=1))

    def middle(u):
        sc, dp, pb, db = scs[u % 2], dps[u % 2], pbs[u % 2], dbs[u % 2]
        for lt in range(HG // 2):
            ls = slice(lt * 2 * TILE, (lt + 1) * 2 * TILE)
            top = jnp.full((8, 2 * TILE), NEG, F32)
            for kb in range(BACK + 1):
                rows = slice(kb * TILE, (kb + 1) * TILE)
                top = jnp.maximum(top, fold(sc[rows, ls], jnp.max))
            top = jnp.max(top, axis=0, keepdims=True) * TO_EXP2
            total = jnp.zeros((8, 2 * TILE), F32)
            inner = jnp.zeros((8, 2 * TILE), F32)
            for kb in range(BACK + 1):
                rows = slice(kb * TILE, (kb + 1) * TILE)
                e = jnp.exp2(sc[rows, ls] * TO_EXP2 - top)
                sc[rows, ls] = e
                total = total + fold(e, jnp.sum)
                inner = inner + fold(e * dp[rows, ls], jnp.sum)
            inv = 1.0 / jnp.sum(total, axis=0, keepdims=True)
            delta = jnp.sum(inner, axis=0, keepdims=True) * inv
            for kb in range(BACK + 1):
                rows = slice(kb * TILE, (kb + 1) * TILE)
                p = sc[rows, ls] * inv
                pb[rows, ls] = p.astype(BF)
                db[rows, ls] = (p * (dp[rows, ls] - delta)).astype(BF)

    def tail(u, q_term):
        turn, h0 = units[u]
        j = h0 // 8
        pb, db = pbs[u % 2], dbs[u % 2]
        keys = pl.ds(bases[turn], WIN)
        dqt = dot(kt[j, :, keys], db[...]) * SCALE
        for i, h in enumerate(range(h0, h0 + HG)):
            cols = slice(h * HD, (h + 1) * HD)
            dn = rope_back(
                dqt[:, i * TILE : (i + 1) * TILE].T, tc[own_rows[turn], :], ts[own_rows[turn], :]
            )
            x = xq[turn, :, cols].astype(F32)
            rs = inv_rms(x)
            q_term = q_term + fold(dn * x * rs, jnp.sum)
            dqs[turn][:, cols] = norm_back(dn, x, rs, qgain).astype(BF)
        mine = slice(h0 * TILE, (h0 + HG) * TILE)
        dv_acc[j, keys, :] += dot(pb[...], g8s[turn, mine, :])
        dk_acc[j, keys, :] += dot(db[...], q8s[turn, mine, :])
        return q_term

    q_term = jnp.zeros((8, HD), F32)
    front(0)
    for u in range(len(units)):
        if u + 1 < len(units):
            front(u + 1)
        middle(u)
        q_term = tail(u, q_term)
    k_term = jnp.zeros((8, HD), F32)
    outs = (out4, out3, out2, out1, own_ref)
    for blk in range(BACK + 2):
        rows = slice(blk * TILE, (blk + 1) * TILE)
        part = slice((blk % 2) * TILE, (blk % 2 + 1) * TILE)
        out = outs[blk // 2]
        for j in range(2):
            dk_cols, dv_cols = slice(j * HD, (j + 1) * HD), slice((2 + j) * HD, (3 + j) * HD)
            dk = dk_acc[j, rows, :] * SCALE
            x = kvs[blk // 2][part, dk_cols].astype(F32)
            dn = rope_back(dk, tc[rows, :], ts[rows, :])
            k_term = k_term + fold(dn * x * inv_rms(x), jnp.sum)
            out[part, dk_cols] = dk.astype(out.dtype)
            out[part, dv_cols] = dv_acc[j, rows, :].astype(out.dtype)
    gains_ref[0:1, :] = jnp.sum(q_term, axis=0, keepdims=True)
    gains_ref[1:2, :] = jnp.sum(k_term, axis=0, keepdims=True)


def finish_kernel(core_ref, own_ref, r1, r2, r3, r4, kv_ref, tc_ref, ts_ref, kg_ref, mine_ref, other_ref, both):
    core = core_ref[0]
    for b in range(2):
        rows = slice(b * TILE, (b + 1) * TILE)
        total = own_ref[rows, :]
        for r in (r1, r2, r3, r4):
            total = total + r[rows, :].astype(F32)
        for j in range(2):
            cols = slice(j * HD, (j + 1) * HD)
            x = kv_ref[rows, cols].astype(F32)
            dn = rope_back(total[:, cols], tc_ref[rows, :], ts_ref[rows, :])
            both[b, :, cols] = norm_back(dn, x, inv_rms(x), kg_ref[...]).astype(BF)
        both[b, :, 2 * HD :] = total[:, 2 * HD :].astype(BF)
    mine_ref[...] = both[core]
    other_ref[...] = both[1 - core]


def head_grads(core1, src, recv, kv4, kv3, kv2, kv1, kv0, grad_out, g_sib, tc, ts, bias, q_gain, k_gain):
    sds = jax.ShapeDtypeStruct
    groups, wide = recv.shape[0] // 2, 16 * HD
    rows2 = 2 * TILE
    unit = HG * TILE
    return pl.pallas_call(
        heads_kernel,
        out_shape=(
            [sds((TILE, wide), BF)] * 2
            + [sds((rows2, 4 * HD), BF)] * 4
            + [sds((rows2, 4 * HD), F32), sds((2, HD), F32)]
        ),
        grid_spec=pltpu.PrefetchScalarGridSpec(
            num_scalar_prefetch=2,
            grid=(1,),
            in_specs=[pl.BlockSpec((2 * groups, RUN, wide), lambda i, c, s: (0, 0, 0))]
            + [whole(rows2, 4 * HD)] * 5
            + [pl.BlockSpec((TILE, wide), lambda i, c, s: (0, c[0]))]
            + [whole(TILE, wide)]
            + [whole(ALLW, HD)] * 2
            + [whole(2, WIN, TILE)]
            + [whole(1, HD)] * 2,
            out_specs=[whole(TILE, wide)] * 2 + [whole(rows2, 4 * HD)] * 5 + [whole(2, HD)],
            scratch_shapes=[
                pltpu.VMEM((2, ALLW, HD), BF),
                pltpu.VMEM((2, HD, ALLW), BF),
                pltpu.VMEM((2, ALLW, HD), BF),
                pltpu.VMEM((2, TILE, wide), BF),
                pltpu.VMEM((2, wide, HD), BF),
                pltpu.VMEM((2, wide, HD), BF),
            ]
            + [pltpu.VMEM((WIN, unit), F32)] * 4
            + [pltpu.VMEM((WIN, unit), BF)] * 4
            + [pltpu.VMEM((2, ALLW, HD), F32)] * 2,
        ),
        compiler_params=ALL_VMEM,
        cost_estimate=pl.CostEstimate(flops=6 * 10**9, bytes_accessed=12 * 10**6, transcendentals=5 * 10**6),
        name="head_grads",
    )(
        core1, src, recv, kv4, kv3, kv2, kv1, kv0, grad_out, g_sib, tc, ts, bias,
        q_gain.reshape(1, HD), k_gain.reshape(1, HD),
    )


def body(q_in, k_in, v_in, grad_out, q_gain, k_gain, shift_plan, segment_ids):
    groups = lax.axis_size("dp")
    chips = lax.axis_size("chip")
    member = lax.axis_index("dp").astype(jnp.int32)
    core = lax.axis_index("core").astype(jnp.int32)
    core1 = core.reshape(1)
    wide = q_in.shape[1] // 2
    rows2 = 2 * TILE
    sds = jax.ShapeDtypeStruct

    def to_sibling(x):
        return lax.ppermute(x, "core", [(0, 1), (1, 0)])

    def ahead(x, d):
        return lax.ppermute(x, "chip", [(i, i + d) for i in range(chips - d)])

    def behind(x, d):
        return lax.ppermute(x, "chip", [(i, i - d) for i in range(d, chips)])

    def by_core(mine, other, axis):
        return jnp.where(
            core == 0,
            jnp.concatenate([mine, other], axis=axis),
            jnp.concatenate([other, mine], axis=axis),
        )

    packed = pl.pallas_call(
        send_kernel,
        out_shape=sds((2 * groups, RUN, 2560), BF),
        grid=(1,),
        in_specs=[SM, SM, whole(*q_in.shape), whole(*k_in.shape), whole(*v_in.shape)],
        out_specs=whole(2 * groups, RUN, 2560),
        compiler_params=ALL_VMEM,
        name="pack_runs",
    )(shift_plan, member.reshape(1), q_in, k_in, v_in)
    recv = lax.all_to_all(packed, ("dp", "core"), 0, 0, tiled=True)
    small = jnp.concatenate([shift_plan, segment_ids + 1], axis=1)
    small2 = by_core(small, to_sibling(small), 0)
    src = 2 * ((member - small2[:, :groups]) % groups) + jnp.arange(2, dtype=jnp.int32)[:, None]
    src = src.reshape(2 * groups)
    ids = small2[:, groups:].reshape(1, rows2)
    id_win = [ahead(ids, d) for d in range(1, 5)]
    half = jnp.arange(HD // 2, dtype=F32)
    freq = THETA ** (-(half * 2.0 / HD))
    freq = jnp.concatenate([freq, freq]).reshape(1, HD)
    tc, ts, bias = pl.pallas_call(
        tables_kernel,
        out_shape=[sds((ALLW, HD), F32), sds((ALLW, HD), F32), sds((2, WIN, TILE), BF)],
        grid=(1,),
        in_specs=[SM] + [whole(1, rows2)] * 5 + [whole(1, HD)],
        out_specs=[whole(ALLW, HD)] * 2 + [whole(2, WIN, TILE)],
        compiler_params=PARAMS,
        name="rope_tables",
    )(core1, *id_win[::-1], ids, freq)
    g_sib = to_sibling(lax.dynamic_slice_in_dim(grad_out, (1 - core) * wide, wide, 1))
    kv0 = pl.pallas_call(
        keys_kernel,
        out_shape=sds((rows2, 4 * HD), BF),
        grid=(1,),
        in_specs=[SM, pl.BlockSpec((2 * groups, RUN, 4 * HD), lambda i: (0, 0, 4))],
        out_specs=whole(rows2, 4 * HD),
        compiler_params=PARAMS,
        name="own_keys",
    )(src, recv)
    kv = [ahead(kv0, d) for d in range(1, 5)]
    dq_mine, dq_other, *parts, own, gains = head_grads(
        core1, src, recv, *kv[::-1], kv0, grad_out, g_sib, tc, ts, bias, q_gain, k_gain
    )
    back = [behind(part, d) for d, part in zip(range(1, 5), parts)]
    dq_got = to_sibling(dq_other)
    gains = gains + to_sibling(gains)
    gains, dq_got = lax.optimization_barrier((gains, dq_got))
    every = groups * chips
    spread = jnp.broadcast_to(gains.reshape(1, 1, 2 * HD), (every, 1, 2 * HD))
    terms = jnp.sum(lax.all_to_all(spread, ("dp", "chip"), 0, 0, tiled=True), axis=(0, 1))
    own, terms = lax.optimization_barrier((own, terms))
    mine, other = pl.pallas_call(
        finish_kernel,
        out_shape=[sds((TILE, 4 * HD), BF)] * 2,
        grid=(1,),
        in_specs=[SM]
        + [whole(rows2, 4 * HD)] * 6
        + [pl.BlockSpec((rows2, HD), lambda i: (BACK // 2, 0))] * 2
        + [whole(1, HD)],
        out_specs=[whole(TILE, 4 * HD)] * 2,
        scratch_shapes=[pltpu.VMEM((2, TILE, 4 * HD), BF)],
        compiler_params=PARAMS,
        name="finish_keys",
    )(core1, own, *back, kv0, tc, ts, k_gain.reshape(1, HD))
    got = to_sibling(other)
    dq = by_core(dq_mine, dq_got, 1)
    dk = by_core(mine[:, : 2 * HD], got[:, : 2 * HD], 1)
    dv = by_core(mine[:, 2 * HD :], got[:, 2 * HD :], 1)
    return dq, dk, dv, terms[:HD], terms[HD:]


def solution(mesh):
    fine = Mesh(mesh.devices.reshape(mesh.shape["dp"], -1, 2), ("dp", "chip", "core"))
    rows = P(("dp", "chip", "core"), None)
    return jax.shard_map(
        body,
        mesh=fine,
        in_specs=(rows, rows, rows, rows, P(), P(), P(("chip", "core"), None), P("dp", ("chip", "core"))),
        out_specs=(rows, rows, rows, P(), P()),
        check_vma=False,
    )
```

```python
import math

import jax
import jax.numpy as jnp
from jax import lax
from jax.experimental import pallas as pl
from jax.experimental.pallas import tpu as pltpu
from jax.sharding import Mesh, PartitionSpec as P

THETA = 1000000.0
EPS = 1e-06
NEG = -1e30
HG = 4
HD = 128
RUN = 16
TILE = 128
BACK = 8
WIN = (BACK + 1) * TILE
ALLW = (BACK + 2) * TILE
SCALE = HD**-0.5
TO_EXP2 = SCALE * math.log2(math.e)
BF = jnp.bfloat16
F32 = jnp.float32
SM = pl.BlockSpec(memory_space=pltpu.SMEM)
PARAMS = pltpu.CompilerParams(vmem_limit_bytes=48 * 1024 * 1024)
ALL_VMEM = pltpu.CompilerParams(vmem_limit_bytes=60 * 1024 * 1024)


def whole(*shape):
    return pl.BlockSpec(shape, lambda i, *scalars: (0,) * len(shape))


def sincos(angle):
    turns = jnp.round(angle * (2.0 / math.pi))
    r = ((angle - turns * 1.5703125) - turns * 4.837512969970703e-4) - turns * 7.549789948768648e-8
    r2 = r * r
    sin_r = r + r * r2 * (-1.6666654611e-1 + r2 * (8.3321608736e-3 - 1.9515295891e-4 * r2))
    cos_r = 1.0 - 0.5 * r2 + r2 * r2 * (
        4.166664568298827e-2 + r2 * (-1.388731625493765e-3 + 2.443315711809948e-5 * r2)
    )
    quarter = turns.astype(jnp.int32)
    swap = (quarter & 1) == 1
    s = jnp.where(swap, cos_r, sin_r)
    c = jnp.where(swap, sin_r, cos_r)
    s = jnp.where((quarter & 2) == 2, -s, s)
    c = jnp.where(((quarter + 1) & 2) == 2, -c, c)
    return s, c


def inv_rms(x):
    return lax.rsqrt(jnp.sum(x * x, axis=-1, keepdims=True) * (1.0 / HD) + EPS)


def rope(x, tc, ts):
    return x * tc + pltpu.roll(x, HD // 2, 1) * ts


def rope_back(x, tc, ts):
    return x * tc - pltpu.roll(x, HD // 2, 1) * ts


def norm_back(dn, x, rs, gain):
    w = dn * gain
    return rs * w - x * (rs * rs * rs) * (jnp.sum(w * x, axis=-1, keepdims=True) * (1.0 / HD))


def fold(x, op):
    return op(x.reshape(x.shape[0] // 8, 8, x.shape[1]), axis=0)


def dot(a, b):
    return jnp.dot(a, b, preferred_element_type=F32)


def send_kernel(plan_ref, who_ref, q_ref, k_ref, v_ref, out_ref):
    groups = plan_ref.shape[1]
    wide_q, wide_k = q_ref.shape[1] // 2, k_ref.shape[1] // 2
    for r in range(groups):
        to = lax.rem(who_ref[0] + plan_ref[0, r], groups)
        rows = slice(r * RUN, (r + 1) * RUN)
        for a in range(2):
            out_ref[2 * to + a, :, :wide_q] = q_ref[rows, a * wide_q : (a + 1) * wide_q]
            out_ref[2 * to + a, :, wide_q : wide_q + wide_k] = k_ref[rows, a * wide_k : (a + 1) * wide_k]
            out_ref[2 * to + a, :, wide_q + wide_k :] = v_ref[rows, a * wide_k : (a + 1) * wide_k]


def keys_kernel(src_ref, recv_ref, out_ref):
    for b in range(2):
        for r in range(8):
            rows = slice(b * TILE + r * RUN, b * TILE + (r + 1) * RUN)
            out_ref[rows, :] = recv_ref[src_ref[b * 8 + r]]


def tables_kernel(core_ref, id4, id3, id2, id1, id0, freq_ref, tc, ts, bias):
    core = core_ref[0]
    lane = lax.broadcasted_iota(jnp.int32, (TILE, TILE), 1)
    sub = lax.broadcasted_iota(jnp.int32, (TILE, TILE), 0)
    subf = sub.astype(F32)
    ids = [jnp.broadcast_to(one[...], (8, 2 * TILE)) for one in (id4, id3, id2, id1, id0)]
    begin = jnp.zeros((8, 2 * TILE), F32)
    for v in range(1, 9):
        less = sum(jnp.where(one < v, 1.0, 0.0) for one in ids)
        begin = begin + jnp.where(ids[-1] == v, jnp.sum(less, axis=1, keepdims=True), 0.0)
    for blk in range(BACK + 2):
        rows = slice(blk * TILE, (blk + 1) * TILE)
        if blk < BACK:
            start = begin[0:1, 0:1]
        else:
            mine = slice((blk - BACK) * TILE, (blk - BACK + 1) * TILE)
            start = jnp.broadcast_to(begin[0:1, mine], (TILE, TILE)).T
        sine, cosine = sincos((subf + float(blk * TILE) - start) * freq_ref[...])
        tc[rows, :] = cosine
        ts[rows, :] = jnp.where(lane < HD // 2, -sine, sine)
    for turn in range(2):
        tile = core if turn == 0 else 1 - core
        st = jnp.where(tile == 0, begin[0:1, :TILE], begin[0:1, TILE:]) - (tile * TILE).astype(F32)
        for kb in range(BACK + 1):
            ok = (subf + float(kb * TILE)) >= st
            if kb == BACK:
                ok = ok & (sub <= lane)
            bias[turn, kb * TILE : (kb + 1) * TILE, :] = jnp.where(ok, 0.0, NEG).astype(BF)


def heads_kernel(
    core_ref, src_ref, recv_ref, kv4, kv3a, kv3b, kv2, kv1, kv0, g_own, g_sib, tc, ts, bias, qg_ref, kg_ref,
    dq_own, dq_sib, out1, out2, out3, out4, own_ref, gains_ref,
    kv3, kr, kt, vs, xq, q8s, g8s, sc0, sc1, dp0, dp1, pb0, pb1, db0, db1, dk_acc, dv_acc,
):
    core = core_ref[0]
    kv3[...] = kv3a[...] + kv3b[...]
    kvs = (kv4, kv3, kv2, kv1, kv0)
    lane = lax.broadcasted_iota(jnp.int32, (TILE, TILE), 1)
    sub = lax.broadcasted_iota(jnp.int32, (TILE, TILE), 0)
    eye = jnp.where(sub == lane, 1.0, 0.0).astype(BF)
    qgain, kgain = qg_ref[...], kg_ref[...]
    for blk in range(BACK + 2):
        rows = slice(blk * TILE, (blk + 1) * TILE)
        ref, part = kvs[blk // 2], slice((blk % 2) * TILE, (blk % 2 + 1) * TILE)
        for j in range(2):
            x = ref[part, j * HD : (j + 1) * HD].astype(F32)
            turned = rope(x * inv_rms(x) * kgain, tc[rows, :], ts[rows, :])
            kr[j, rows, :] = turned.astype(BF)
            kt[j, :, rows] = turned.T.astype(BF)
            vs[j, rows, :] = ref[part, (2 + j) * HD : (3 + j) * HD]
    dk_acc[...] = jnp.zeros_like(dk_acc)
    dv_acc[...] = jnp.zeros_like(dv_acc)
    bases, own_rows = [], []
    for turn in range(2):
        tile = core if turn == 0 else 1 - core
        base = pl.multiple_of(tile * TILE, TILE)
        bases.append(base)
        own_rows.append(pl.ds(pl.multiple_of(BACK * TILE + base, TILE), TILE))
        for r in range(8):
            xq[turn, r * RUN : (r + 1) * RUN, :] = recv_ref[src_ref[tile * 8 + r]]
    gs, dqs = (g_own, g_sib), (dq_own, dq_sib)
    scs, dps, pbs, dbs = (sc0, sc1), (dp0, dp1), (pb0, pb1), (db0, db1)
    units = [(turn, h) for turn in range(2) for h in range(0, 16, HG)]

    def front(u):
        turn, h0 = units[u]
        j, qts, gts = h0 // 8, [], []
        for h in range(h0, h0 + HG):
            cols = slice(h * HD, (h + 1) * HD)
            x = xq[turn, :, cols].astype(F32)
            turned = rope(x * inv_rms(x) * qgain, tc[own_rows[turn], :], ts[own_rows[turn], :])
            grad = gs[turn][:, cols]
            q8s[turn, h * TILE : (h + 1) * TILE, :] = turned.astype(BF)
            g8s[turn, h * TILE : (h + 1) * TILE, :] = grad
            qts.append(turned.T.astype(BF))
            gts.append(grad.astype(F32).T.astype(BF))
        qt = jnp.concatenate(
            [jnp.concatenate(qts, axis=1), jnp.concatenate([eye] * HG, axis=1)], axis=0
        )
        win = pl.ds(bases[turn], WIN)
        scs[u % 2][...] = dot(jnp.concatenate([kr[j, win, :], bias[turn]], axis=1), qt)
        dps[u % 2][...] = dot(vs[j, win, :], jnp.concatenate(gts, axis=1))

    def middle(u):
        sc, dp, pb, db = scs[u % 2], dps[u % 2], pbs[u % 2], dbs[u % 2]
        for lt in range(HG // 2):
            ls = slice(lt * 2 * TILE, (lt + 1) * 2 * TILE)
            top = jnp.full((8, 2 * TILE), NEG, F32)
            for kb in range(BACK + 1):
                rows = slice(kb * TILE, (kb + 1) * TILE)
                top = jnp.maximum(top, fold(sc[rows, ls], jnp.max))
            top = jnp.max(top, axis=0, keepdims=True) * TO_EXP2
            total = jnp.zeros((8, 2 * TILE), F32)
            inner = jnp.zeros((8, 2 * TILE), F32)
            for kb in range(BACK + 1):
                rows = slice(kb * TILE, (kb + 1) * TILE)
                e = jnp.exp2(sc[rows, ls] * TO_EXP2 - top)
                sc[rows, ls] = e
                total = total + fold(e, jnp.sum)
                inner = inner + fold(e * dp[rows, ls], jnp.sum)
            inv = 1.0 / jnp.sum(total, axis=0, keepdims=True)
            delta = jnp.sum(inner, axis=0, keepdims=True) * inv
            for kb in range(BACK + 1):
                rows = slice(kb * TILE, (kb + 1) * TILE)
                p = sc[rows, ls] * inv
                pb[rows, ls] = p.astype(BF)
                db[rows, ls] = (p * (dp[rows, ls] - delta)).astype(BF)

    def tail(u, q_term):
        turn, h0 = units[u]
        j = h0 // 8
        pb, db = pbs[u % 2], dbs[u % 2]
        keys = pl.ds(bases[turn], WIN)
        dqt = dot(kt[j, :, keys], db[...]) * SCALE
        for i, h in enumerate(range(h0, h0 + HG)):
            cols = slice(h * HD, (h + 1) * HD)
            dn = rope_back(
                dqt[:, i * TILE : (i + 1) * TILE].T, tc[own_rows[turn], :], ts[own_rows[turn], :]
            )
            x = xq[turn, :, cols].astype(F32)
            rs = inv_rms(x)
            q_term = q_term + fold(dn * x * rs, jnp.sum)
            dqs[turn][:, cols] = norm_back(dn, x, rs, qgain).astype(BF)
        mine = slice(h0 * TILE, (h0 + HG) * TILE)
        dv_acc[j, keys, :] += dot(pb[...], g8s[turn, mine, :])
        dk_acc[j, keys, :] += dot(db[...], q8s[turn, mine, :])
        return q_term

    q_term = jnp.zeros((8, HD), F32)
    front(0)
    for u in range(len(units)):
        if u + 1 < len(units):
            front(u + 1)
        middle(u)
        q_term = tail(u, q_term)
    k_term = jnp.zeros((8, HD), F32)
    outs = (out4, out3, out2, out1, own_ref)
    for blk in range(BACK + 2):
        rows = slice(blk * TILE, (blk + 1) * TILE)
        part = slice((blk % 2) * TILE, (blk % 2 + 1) * TILE)
        out = outs[blk // 2]
        for j in range(2):
            dk_cols, dv_cols = slice(j * HD, (j + 1) * HD), slice((2 + j) * HD, (3 + j) * HD)
            dk = dk_acc[j, rows, :] * SCALE
            x = kvs[blk // 2][part, dk_cols].astype(F32)
            dn = rope_back(dk, tc[rows, :], ts[rows, :])
            k_term = k_term + fold(dn * x * inv_rms(x), jnp.sum)
            out[part, dk_cols] = dk.astype(out.dtype)
            out[part, dv_cols] = dv_acc[j, rows, :].astype(out.dtype)
    gains_ref[0:1, :] = jnp.sum(q_term, axis=0, keepdims=True)
    gains_ref[1:2, :] = jnp.sum(k_term, axis=0, keepdims=True)


def finish_kernel(core_ref, own_ref, r1, r2, r3, r4, kv_ref, tc_ref, ts_ref, kg_ref, mine_ref, other_ref, both):
    core = core_ref[0]
    for b in range(2):
        rows = slice(b * TILE, (b + 1) * TILE)
        total = own_ref[rows, :]
        for r in (r1, r2, r3, r4):
            total = total + r[rows, :].astype(F32)
        for j in range(2):
            cols = slice(j * HD, (j + 1) * HD)
            x = kv_ref[rows, cols].astype(F32)
            dn = rope_back(total[:, cols], tc_ref[rows, :], ts_ref[rows, :])
            both[b, :, cols] = norm_back(dn, x, inv_rms(x), kg_ref[...]).astype(BF)
        both[b, :, 2 * HD :] = total[:, 2 * HD :].astype(BF)
    mine_ref[...] = both[core]
    other_ref[...] = both[1 - core]


def head_grads(core1, src, recv, kv4, kv3, kv3r, kv2, kv1, kv0, grad_out, g_sib, tc, ts, bias, q_gain, k_gain):
    sds = jax.ShapeDtypeStruct
    groups, wide = recv.shape[0] // 2, 16 * HD
    rows2 = 2 * TILE
    unit = HG * TILE
    return pl.pallas_call(
        heads_kernel,
        out_shape=(
            [sds((TILE, wide), BF)] * 2
            + [sds((rows2, 4 * HD), BF)] * 4
            + [sds((rows2, 4 * HD), F32), sds((2, HD), F32)]
        ),
        grid_spec=pltpu.PrefetchScalarGridSpec(
            num_scalar_prefetch=2,
            grid=(1,),
            in_specs=[pl.BlockSpec((2 * groups, RUN, wide), lambda i, c, s: (0, 0, 0))]
            + [whole(rows2, 4 * HD)] * 6
            + [pl.BlockSpec((TILE, wide), lambda i, c, s: (0, c[0]))]
            + [whole(TILE, wide)]
            + [whole(ALLW, HD)] * 2
            + [whole(2, WIN, TILE)]
            + [whole(1, HD)] * 2,
            out_specs=[whole(TILE, wide)] * 2 + [whole(rows2, 4 * HD)] * 5 + [whole(2, HD)],
            scratch_shapes=[
                pltpu.VMEM((rows2, 4 * HD), BF),
                pltpu.VMEM((2, ALLW, HD), BF),
                pltpu.VMEM((2, HD, ALLW), BF),
                pltpu.VMEM((2, ALLW, HD), BF),
                pltpu.VMEM((2, TILE, wide), BF),
                pltpu.VMEM((2, wide, HD), BF),
                pltpu.VMEM((2, wide, HD), BF),
            ]
            + [pltpu.VMEM((WIN, unit), F32)] * 4
            + [pltpu.VMEM((WIN, unit), BF)] * 4
            + [pltpu.VMEM((2, ALLW, HD), F32)] * 2,
        ),
        compiler_params=ALL_VMEM,
        cost_estimate=pl.CostEstimate(flops=6 * 10**9, bytes_accessed=12 * 10**6, transcendentals=5 * 10**6),
        name="head_grads",
    )(
        core1, src, recv, kv4, kv3, kv3r, kv2, kv1, kv0, grad_out, g_sib, tc, ts, bias,
        q_gain.reshape(1, HD), k_gain.reshape(1, HD),
    )


def body(q_in, k_in, v_in, grad_out, q_gain, k_gain, shift_plan, segment_ids):
    groups = lax.axis_size("dp")
    chips = lax.axis_size("chip")
    member = lax.axis_index("dp").astype(jnp.int32)
    core = lax.axis_index("core").astype(jnp.int32)
    core1 = core.reshape(1)
    wide = q_in.shape[1] // 2
    rows2 = 2 * TILE
    sds = jax.ShapeDtypeStruct

    def to_sibling(x):
        return lax.ppermute(x, "core", [(0, 1), (1, 0)])

    def ahead(x, d):
        return lax.ppermute(x, "chip", [(i, i + d) for i in range(chips - d)])

    def behind(x, d):
        return lax.ppermute(x, "chip", [(i, i - d) for i in range(d, chips)])

    def by_core(mine, other, axis):
        return jnp.where(
            core == 0,
            jnp.concatenate([mine, other], axis=axis),
            jnp.concatenate([other, mine], axis=axis),
        )

    packed = pl.pallas_call(
        send_kernel,
        out_shape=sds((2 * groups, RUN, 2560), BF),
        grid=(1,),
        in_specs=[SM, SM, whole(*q_in.shape), whole(*k_in.shape), whole(*v_in.shape)],
        out_specs=whole(2 * groups, RUN, 2560),
        compiler_params=ALL_VMEM,
        name="pack_runs",
    )(shift_plan, member.reshape(1), q_in, k_in, v_in)
    recv = lax.all_to_all(packed, ("dp", "core"), 0, 0, tiled=True)
    small = jnp.concatenate([shift_plan, segment_ids + 1], axis=1)
    small2 = by_core(small, to_sibling(small), 0)
    src = 2 * ((member - small2[:, :groups]) % groups) + jnp.arange(2, dtype=jnp.int32)[:, None]
    src = src.reshape(2 * groups)
    ids = small2[:, groups:].reshape(1, rows2)
    id_win = [ahead(ids, d) for d in range(1, 5)]
    half = jnp.arange(HD // 2, dtype=F32)
    freq = THETA ** (-(half * 2.0 / HD))
    freq = jnp.concatenate([freq, freq]).reshape(1, HD)
    tc, ts, bias = pl.pallas_call(
        tables_kernel,
        out_shape=[sds((ALLW, HD), F32), sds((ALLW, HD), F32), sds((2, WIN, TILE), BF)],
        grid=(1,),
        in_specs=[SM] + [whole(1, rows2)] * 5 + [whole(1, HD)],
        out_specs=[whole(ALLW, HD)] * 2 + [whole(2, WIN, TILE)],
        compiler_params=PARAMS,
        name="rope_tables",
    )(core1, *id_win[::-1], ids, freq)
    g_sib = to_sibling(lax.dynamic_slice_in_dim(grad_out, (1 - core) * wide, wide, 1))
    recv, tc, ts, bias = lax.optimization_barrier((recv, tc, ts, bias))
    kv0 = pl.pallas_call(
        keys_kernel,
        out_shape=sds((rows2, 4 * HD), BF),
        grid=(1,),
        in_specs=[SM, pl.BlockSpec((2 * groups, RUN, 4 * HD), lambda i: (0, 0, 4))],
        out_specs=whole(rows2, 4 * HD),
        compiler_params=PARAMS,
        name="own_keys",
    )(src, recv)
    kv = {d: ahead(kv0, d) for d in (4, 2, 1)}
    straight = lax.ppermute(kv0, "chip", [(i, i + 3) for i in range(0, chips - 3, 2)])
    relayed = lax.ppermute(kv[4], "chip", [(i + 1, i) for i in range(4, chips, 2)])
    dq_mine, dq_other, *parts, own, gains = head_grads(
        core1, src, recv, kv[4], straight, relayed, kv[2], kv[1], kv0, grad_out, g_sib, tc, ts, bias, q_gain, k_gain
    )
    back = [behind(part, d) for d, part in zip(range(1, 5), parts)]
    dq_got = to_sibling(dq_other)
    gains = gains + to_sibling(gains)
    gains, dq_got = lax.optimization_barrier((gains, dq_got))
    every = groups * chips
    spread = jnp.broadcast_to(gains.reshape(1, 1, 2 * HD), (every, 1, 2 * HD))
    terms = jnp.sum(lax.all_to_all(spread, ("dp", "chip"), 0, 0, tiled=True), axis=(0, 1))
    own, terms = lax.optimization_barrier((own, terms))
    mine, other = pl.pallas_call(
        finish_kernel,
        out_shape=[sds((TILE, 4 * HD), BF)] * 2,
        grid=(1,),
        in_specs=[SM]
        + [whole(rows2, 4 * HD)] * 6
        + [pl.BlockSpec((rows2, HD), lambda i: (BACK // 2, 0))] * 2
        + [whole(1, HD)],
        out_specs=[whole(TILE, 4 * HD)] * 2,
        scratch_shapes=[pltpu.VMEM((2, TILE, 4 * HD), BF)],
        compiler_params=PARAMS,
        name="finish_keys",
    )(core1, own, *back, kv0, tc, ts, k_gain.reshape(1, HD))
    got = to_sibling(other)
    dq = by_core(dq_mine, dq_got, 1)
    dk = by_core(mine[:, : 2 * HD], got[:, : 2 * HD], 1)
    dv = by_core(mine[:, 2 * HD :], got[:, 2 * HD :], 1)
    return dq, dk, dv, terms[:HD], terms[HD:]


def solution(mesh):
    fine = Mesh(mesh.devices.reshape(mesh.shape["dp"], -1, 2), ("dp", "chip", "core"))
    rows = P(("dp", "chip", "core"), None)
    return jax.shard_map(
        body,
        mesh=fine,
        in_specs=(rows, rows, rows, rows, P(), P(), P(("chip", "core"), None), P("dp", ("chip", "core"))),
        out_specs=(rows, rows, rows, P(), P()),
        check_vma=False,
    )
```
